32 devices in a mesh: groups: 2 (over x), wide: 4 (over y, core), narrow: 4 (over z).
Axes of the slice: x: 2, y: 2, z: 4, core: 2. Of those that a mesh axis runs over, the one named last changes fastest.
Arguments:
- activations: bfloat16 [8, 128, 8192], P('groups', 'wide', 'narrow'), parts along dimension 0, may hold values from -6 to 6
- out_grads: bfloat16 [8, 128, 16384], P('groups', 'narrow', 'wide'), parts along dimension 0, may hold values from -6 to 6
- sign_bits: int32 [512, 16384], P('narrow', 'wide'), may hold values from 0 to 65535
- kept_row: int32 [4096], replicated, may hold values from 0 to 8191
- kept_col: int32 [4096], replicated, may hold values from 0 to 16383
Outputs:
- sketch: float32 [8, 4096], P('groups', ('wide', 'narrow')), parts along dimension 0
The draws below stay inside these ranges and needn't reach their ends.
There are 2 independent parts, one for each index of `groups`. The reference program is written for one: setup_inputs(seed, part) draws one part's arguments, and reference() takes and returns one part's arrays. A program takes and returns all parts, laid end to end along the dimension named above; an argument that names none is the same for every part. Nothing has to cross between parts.
All inputs are finite; a program needn't handle non-finite values.
Results may differ from the reference program's by a relative error of at most 0.005.
Values may be sent and summed in bfloat16 or wider, within the bound.
No kernel may reach another device: no remote copies, remote signals or barrier semaphores. Data moves between devices by JAX's collectives and lax.ppermute only.
A program may use at most 512 MiB of HBM per device.

```python
import math
import jax
import jax.numpy as jnp
from jax import lax

D = 8192
FF = 16384
K = 4096
HLOW = 128
EX = 4
SEQ = 128


def touch_ends(array, own_key, least, largest):
    spot = [jax.random.randint(jax.random.fold_in(own_key, axis), (), 0, length) for axis, length in enumerate(array.shape)]
    widest = array.shape.index(max(array.shape))
    next_to = spot[:widest] + [(spot[widest] + 1) % array.shape[widest]] + spot[widest + 1:]
    return array.at[tuple(spot)].set(least).at[tuple(next_to)].set(largest)


def levels(key, extent, split, least, top_value):
    factor_of = 1.0
    for position, parts in split:
        steps = jax.random.uniform(jax.random.fold_in(jax.random.fold_in(key, 6), position), (parts,), jnp.float32, least / len(split), top_value / len(split))
        factor_of = factor_of * jnp.repeat(jnp.exp(steps), extent[position] // parts).reshape((-1,) + (1,) * (len(extent) - 1 - position))
    return factor_of


def normal_values(own_key, extent, scale, reach, shards=(), kind=jnp.bfloat16):
    drawn = scale * jax.random.normal(own_key, extent, jnp.float32)
    if shards:
        drawn = drawn * levels(own_key, extent, shards, -0.22, 0.18)
    return jnp.clip(drawn, -reach, reach).astype(kind)


def setup_inputs(seed: int = 0, part: int = 0) -> dict:
    key_of = jax.random.split(jax.random.key(seed), 6)
    part_splits = jax.random.split(jax.random.fold_in(key_of[5], part), 6)
    return {
        "activations": normal_values(part_splits[0], (EX, SEQ, D), 1.0, 6.0, ((1, 4), (2, 4))),
        "out_grads": normal_values(part_splits[1], (EX, SEQ, FF), 1.0, 6.0, ((1, 4), (2, 4))),
        "sign_bits": touch_ends(jax.random.randint(key_of[2], (D // 16, FF), 0, 65536), jax.random.fold_in(key_of[2], 1), 0, 65535).astype(jnp.int32),
        "kept_row": touch_ends(jax.random.randint(key_of[3], (K,), 0, D), jax.random.fold_in(key_of[3], 1), 0, D - 1).astype(jnp.int32),
        "kept_col": touch_ends(jax.random.randint(key_of[4], (K,), 0, FF), jax.random.fold_in(key_of[4], 1), 0, FF - 1).astype(jnp.int32),
    }


def parity_sign(first, second):
    folded = first & second
    folded = folded ^ folded >> 16
    folded = folded ^ folded >> 8
    folded = folded ^ folded >> 4
    folded = folded ^ folded >> 2
    folded = folded ^ folded >> 1
    return (1 - 2 * (folded & 1)).astype(jnp.float32)

def sylvester(order):
    index = jnp.arange(order, dtype=jnp.int32)
    return parity_sign(index[:, None], index[None, :])

def reference(activations, out_grads, sign_bits, kept_row, kept_col):
    block_rows = min(1024, D)
    blocks = D // block_rows
    row_high = block_rows // HLOW
    col_high = FF // HLOW
    h_low = sylvester(HLOW).astype(jnp.bfloat16)
    shifts = jnp.arange(16, dtype=jnp.int32)
    row_lowbits = kept_row % HLOW
    row_highbits = kept_row // HLOW
    col_lowbits = kept_col % HLOW
    col_highbits = kept_col // HLOW
    col_coeff = parity_sign(col_highbits[:, None], jnp.arange(col_high, dtype=jnp.int32)[None, :])

    def one_example(pair):
        tokens, grads_out = pair

        def one_block(block):
            start = (block * block_rows).astype(jnp.int32)
            rows_x = lax.dynamic_slice_in_dim(tokens, start, block_rows, 1).astype(jnp.float32)
            grad = jnp.dot(rows_x.T, grads_out.astype(jnp.float32), preferred_element_type=jnp.float32)
            words = lax.dynamic_slice_in_dim(sign_bits, (block * (block_rows // 16)).astype(jnp.int32), block_rows // 16, 0)
            bits = (jnp.right_shift(words[:, None, :], shifts[None, :, None]) & 1).reshape(block_rows, FF)
            signed = ((1.0 - 2.0 * bits.astype(jnp.float32)) * grad).astype(jnp.bfloat16)
            colmix = jnp.einsum('rhl,lm->rhm', signed.reshape(block_rows, col_high, HLOW), h_low, preferred_element_type=jnp.float32).astype(jnp.bfloat16)
            rowmix = jnp.einsum('aqhm,sq->ashm', colmix.reshape(row_high, HLOW, col_high, HLOW), h_low, preferred_element_type=jnp.float32).astype(jnp.bfloat16)
            picked = rowmix[:, row_lowbits, :, col_lowbits].astype(jnp.float32)
            row_ids = block * row_high + jnp.arange(row_high, dtype=jnp.int32)
            row_coeff = parity_sign(row_highbits[:, None], row_ids[None, :])
            return lax.optimization_barrier(jnp.sum(picked * row_coeff[:, :, None] * col_coeff[:, None, :], axis=(1, 2)))
        return lax.optimization_barrier(jnp.sum(lax.map(one_block, jnp.arange(blocks, dtype=jnp.int32)), axis=0))
    sums = lax.map(one_example, (activations, out_grads))
    return sums * (1.0 / math.sqrt(D * FF * SEQ))
```

```python
import functools
import math

import jax
import jax.numpy as jnp
from jax import lax
from jax.experimental import pallas as pl
from jax.experimental.pallas import tpu as pltpu
from jax.sharding import PartitionSpec as P

D = 8192
FF = 16384
SEQ = 128
BLK = 256
LOW = 8
GROUPS = BLK // LOW
LANES = 128
TILE = 128
WIDE = 512
ROW_HIGH = (D // BLK).bit_length() - 1
COL_BITS = FF.bit_length() - 1


def parity_sign(first, second):
    folded = first & second
    folded = folded ^ folded >> 8
    folded = folded ^ folded >> 4
    folded = folded ^ folded >> 2
    folded = folded ^ folded >> 1
    return (1 - 2 * (folded & 1)).astype(jnp.bfloat16)


def in_groups(kept_row, kept_col):
    key = ((kept_row & (BLK - 1)) << ROW_HIGH | kept_row // BLK) << COL_BITS | kept_col
    return lax.sort((key, lax.iota(jnp.int32, key.shape[0])), num_keys=1)


def plan(key, order, base, na, nh):
    k = key.shape[0]
    col = key & (FF - 1)
    row_low = key >> (COL_BITS + ROW_HIGH)
    group = row_low // LOW
    code = (key >> COL_BITS) & (D // BLK - 1) | (col // BLK) << ROW_HIGH
    d = jnp.arange(LANES, dtype=jnp.int32)

    def bits_of(d):
        return (d // LOW) % na | d // (LOW * na) << ROW_HIGH

    hit = (row_low & (LOW - 1))[:, None] == (d % LOW)[None, :]
    pick = jnp.where(hit, parity_sign(code[:, None], (base ^ bits_of(d))[None, :]), 0).astype(jnp.bfloat16)
    tops = (na * nh * LOW // LANES).bit_length() - 1
    top = bits_of(LANES << jnp.arange(max(tops, 1), dtype=jnp.int32))
    flip = jnp.broadcast_to(parity_sign(code[None, :], top[:, None])[:, :, None], (max(tops, 1), k, LANES))
    lane = parity_sign((col & (BLK - 1))[:, None], jnp.arange(BLK, dtype=jnp.int32)[None, :])
    tiles = k // TILE
    low_hot = ((order % LANES)[:, None] == d[None, :]).astype(jnp.bfloat16)
    high = jnp.arange(k // LANES, dtype=jnp.int32)
    high_hot = ((order // LANES)[None, :] == high[:, None]).astype(jnp.bfloat16)
    ends = jnp.sum((group[None, :] <= jnp.arange(GROUPS, dtype=jnp.int32)[:, None]).astype(jnp.int32), axis=1)
    cuts = jnp.sort(jnp.concatenate([jnp.arange(tiles, dtype=jnp.int32) * TILE, ends[:-1]]))
    item_tile = jnp.minimum(cuts // TILE, tiles - 1)
    item_group = jnp.minimum(jnp.sum((ends[None, :] <= cuts[:, None]).astype(jnp.int32), axis=1), GROUPS - 1)
    items = jnp.stack([item_tile, item_group, cuts - item_tile * TILE])
    return items, pick, flip, lane, low_hot, high_hot


def halve(x):
    coarse = x.astype(jnp.bfloat16)
    return coarse, (x - coarse.astype(jnp.float32)).astype(jnp.bfloat16)


def body(parts, na, nc, steps, tops, unroll, items, place, a_ref, *refs):
    g_refs = refs[:parts]
    words_ref, h_ref, pick_hbm, flip_hbm, lane_hbm, low_hbm, high_ref, out_ref, at, w, pick, flip, lane, low, part, spread, sems = refs[parts:]
    step = pl.program_id(0)
    pairs = ((pick_hbm, pick), (flip_hbm, flip), (lane_hbm, lane), (low_hbm, low))
    copies = [pltpu.make_async_copy(s, d, sems.at[i]) for i, (s, d) in enumerate(pairs)]

    @pl.when(step == 0)
    def _():
        for c in copies:
            c.start()
        blocks, _, _, span = a_ref.shape
        for j in range(blocks):
            tokens = jnp.concatenate([a_ref[j, place[0] ^ s] for s in range(parts)], axis=0)
            at[j * span:(j + 1) * span, :] = tokens.T

    depth = na * LOW
    shift = 31 - lax.broadcasted_iota(jnp.int32, (BLK // 16, 16, BLK), 1)
    for c in range(nc):
        cols = slice(c * BLK, (c + 1) * BLK)
        grads_out = jnp.concatenate([g[:, cols] for g in g_refs], axis=0)
        for a in range(0, na, 2):
            halves = []
            for b in (a, a + 1):
                rows = slice(b * BLK, (b + 1) * BLK)
                grad = jnp.dot(at[rows, :], grads_out, preferred_element_type=jnp.float32)
                words = words_ref[b * BLK // 16:(b + 1) * BLK // 16, cols]
                marks = (jnp.broadcast_to(words[:, None, :], shift.shape) << shift).reshape(BLK, BLK)
                signed = jnp.where(marks < 0, -grad, grad).astype(jnp.bfloat16)
                mixed = jnp.dot(h_ref[...], signed, preferred_element_type=jnp.float32)
                halves.append(mixed.reshape(GROUPS, LOW, BLK))
            both = jnp.concatenate(halves, axis=1).astype(jnp.bfloat16)
            w[:, pl.ds(pl.multiple_of((step * nc + c) * depth + a * LOW, 2 * LOW), 2 * LOW), :] = both

    @pl.when(step == steps - 1)
    def _():
        for c in copies:
            c.wait()
        slot = lax.broadcasted_iota(jnp.int32, (TILE, LANES), 0)

        def item(i, carry):
            t, g = items[0, i], items[1, i]
            at_t = pl.ds(pl.multiple_of(t * TILE, TILE), TILE)
            signs = [pick[at_t, :]]
            for b in range(tops):
                signs += [s * flip[b, at_t, :] for s in signs]
            mixed = jnp.dot(jnp.concatenate(signs, axis=1), w[g], preferred_element_type=jnp.float32)
            mixed = mixed * lane[at_t, :].astype(jnp.float32)
            part[at_t, :] = jnp.where(slot >= items[2, i], mixed[:, :LANES] + mixed[:, LANES:], part[at_t, :])
            return carry

        lax.fori_loop(0, items.shape[1], item, 0, unroll=unroll)
        ones = jnp.ones((LANES, LANES), jnp.bfloat16)

        def back(t, carry):
            at_t = pl.ds(pl.multiple_of(t * TILE, TILE), TILE)
            value = sum(jnp.dot(x, ones, preferred_element_type=jnp.float32) for x in halve(part[at_t, :]))
            for i, x in enumerate(halve(value)):
                spread[i, at_t, :] = x * low[at_t, :]
            return carry

        lax.fori_loop(0, high_ref.shape[1] // TILE, back, 0, unroll=32)
        out_ref[...] = sum(jnp.dot(high_ref[...], spread[i], preferred_element_type=jnp.float32) for i in (0, 1))


def sketch_terms(items, place, a, example, g_parts, words, h, pick, flip, lane, low_hot, high_hot):
    blocks, parts, few, span = a.shape
    rows, cols = 16 * words.shape[0], words.shape[1]
    wide = min(cols, WIDE)
    steps = cols // wide
    na, nc = rows // BLK, wide // BLK
    k = pick.shape[0]
    depth = na * nc * steps * LOW
    tops = (depth // LANES).bit_length() - 1
    whole = lambda *shape: pl.BlockSpec(shape, lambda j, *s: (0,) * len(shape))
    hbm = pl.BlockSpec(memory_space=pl.ANY)
    return pl.pallas_call(
        functools.partial(body, parts, na, nc, steps, tops, 21),
        out_shape=jax.ShapeDtypeStruct((k // LANES, LANES), jnp.float32),
        grid_spec=pltpu.PrefetchScalarGridSpec(
            num_scalar_prefetch=2,
            grid=(steps,),
            in_specs=[whole(*a.shape)]
            + [pl.BlockSpec((None, few, wide), lambda j, *s: (example, 0, j))] * parts
            + [pl.BlockSpec((rows // 16, wide), lambda j, *s: (0, j)), whole(BLK, BLK)]
            + [hbm] * 4
            + [whole(*high_hot.shape)],
            out_specs=whole(k // LANES, LANES),
            scratch_shapes=[
                pltpu.VMEM((rows, a.shape[1] * few), jnp.bfloat16),
                pltpu.VMEM((GROUPS, depth, BLK), jnp.bfloat16),
                pltpu.VMEM(pick.shape, jnp.bfloat16),
                pltpu.VMEM(flip.shape, jnp.bfloat16),
                pltpu.VMEM(lane.shape, jnp.bfloat16),
                pltpu.VMEM(low_hot.shape, jnp.bfloat16),
                pltpu.VMEM((k, LANES), jnp.float32),
                pltpu.VMEM((2, k, LANES), jnp.bfloat16),
                pltpu.SemaphoreType.DMA((4,)),
            ],
        ),
        compiler_params=pltpu.CompilerParams(vmem_limit_bytes=52 << 20),
        cost_estimate=pl.CostEstimate(
            flops=2 * rows * wide * steps * 3 * BLK, bytes_accessed=2 * rows * wide * steps, transcendentals=0
        ),
    )(items, place, a, *g_parts, words, h, pick, flip, lane, low_hot, high_hot)


def local(sizes, share, activations, out_grads, sign_bits, kept_row, kept_col):
    wide_size, narrow_size = sizes["wide"], sizes["narrow"]
    n = lax.axis_index("narrow")
    wide_idx = lax.axis_index("wide")
    count = activations.shape[0]
    row_len = activations.shape[2]
    col_len = out_grads.shape[2] // share
    few = out_grads.shape[1]
    k = kept_row.shape[0]
    na = share * row_len // BLK
    nh = col_len // BLK

    def swap(x, s):
        return lax.ppermute(x, "narrow", [(j, j ^ s) for j in range(narrow_size)])

    def columns(x, s):
        return lax.dynamic_slice_in_dim(x, ((n ^ s) % share) * col_len, col_len, x.ndim - 1)

    def panel(shards):
        return lax.all_gather(jnp.stack(shards), "wide", axis=1, tiled=True)

    near = [activations[0]] + [swap(activations[0], s) for s in range(1, share)]
    panels = [panel(near)]
    words = [columns(sign_bits, 0)] + [swap(columns(sign_bits, s).astype(jnp.uint16), s) for s in range(1, share)]
    outs = out_grads[:1]
    grads = [(0, [columns(outs, 0)] + [swap(columns(outs, s), s) for s in range(1, narrow_size)])]
    key, order = in_groups(kept_row, kept_col)
    acts, outs, key, order, *_ = lax.optimization_barrier(
        (activations[1:], out_grads[1:], key, order, words[-1], near[-1])
    )
    words = jnp.concatenate([x.astype(jnp.int32) for x in words])
    others = [acts] + [swap(acts, s) for s in range(1, share)]
    rest = [columns(outs, 0)] + [swap(columns(outs, s), s) for s in range(1, narrow_size)]
    for e in range(count - 1):
        panels.append(panel([x[e] for x in others]))
        grads.append((e, rest))
    base = n * (row_len // BLK) | ((wide_idx * share + n % share) * nh) << ROW_HIGH
    factors = plan(key, order, base, na, nh)
    index = jnp.arange(BLK, dtype=jnp.int32)
    h = parity_sign(index[:, None], index[None, :])
    place = jnp.full((1,), n, jnp.int32)
    terms = []
    for e in range(count):
        a = panels[e].reshape(share, narrow_size, few, row_len)
        terms.append(sketch_terms(factors[0], place, a, *grads[e], words, h, *factors[1:]))
    owners = wide_size * narrow_size
    send = jnp.stack(terms).reshape(count, owners, k // owners).transpose(1, 0, 2)
    got = lax.all_to_all(send, ("wide", "narrow"), 0, 0, tiled=True)
    return jnp.sum(got, axis=0) * (1.0 / math.sqrt(D * FF * SEQ))


def solution(mesh):
    return jax.shard_map(
        functools.partial(local, dict(mesh.shape), 2),
        mesh=mesh,
        in_specs=(
            P("groups", "wide", "narrow"),
            P("groups", "narrow", "wide"),
            P("narrow", "wide"),
            P(),
            P(),
        ),
        out_specs=P("groups", ("wide", "narrow")),
        check_vma=False,
    )
```

```python
import functools
import math

import jax
import jax.numpy as jnp
from jax import lax
from jax.experimental import pallas as pl
from jax.experimental.pallas import tpu as pltpu
from jax.sharding import PartitionSpec as P

D = 8192
FF = 16384
SEQ = 128
BLK = 256
LOW = 8
GROUPS = BLK // LOW
LANES = 128
TILE = 128
WIDE = 512
ROW_HIGH = (D // BLK).bit_length() - 1
COL_BITS = FF.bit_length() - 1


def parity_sign(first, second):
    folded = first & second
    folded = folded ^ folded >> 8
    folded = folded ^ folded >> 4
    folded = folded ^ folded >> 2
    folded = folded ^ folded >> 1
    return (1 - 2 * (folded & 1)).astype(jnp.bfloat16)


def in_groups(kept_row, kept_col):
    key = ((kept_row & (BLK - 1)) << ROW_HIGH | kept_row // BLK) << COL_BITS | kept_col
    return lax.sort((key, lax.iota(jnp.int32, key.shape[0])), num_keys=1)


def factor_body(na, tops, base, key_ref, order_ref, pick, flip, lane, low, high):
    d = lax.broadcasted_iota(jnp.int32, (TILE, LANES), 1)
    low_bits = LOW.bit_length() - 1
    na_bits = na.bit_length() - 1
    place = base[0] ^ ((d >> low_bits) & (na - 1) | d >> (low_bits + na_bits) << ROW_HIGH)
    coarse = lax.broadcasted_iota(jnp.int32, (high.shape[0], LANES), 0)

    def down(ref, t):
        return jnp.broadcast_to(ref[pl.ds(t, 1), :], (TILE, LANES)).T

    def sign(odd):
        return (1 - 2 * (odd & 1)).astype(jnp.float32)

    def tile(t, carry):
        at_t = pl.ds(pl.multiple_of(t * TILE, TILE), TILE)
        key = down(key_ref, t)
        col = key & (FF - 1)
        row_low = key >> (COL_BITS + ROW_HIGH)
        code = (key >> COL_BITS) & (D // BLK - 1) | col // BLK << ROW_HIGH
        odd = code & place
        for b in (8, 4, 2, 1):
            odd = odd ^ odd >> b
        pick[at_t, :] = jnp.where((row_low ^ d) & (LOW - 1) == 0, sign(odd), 0.0).astype(jnp.bfloat16)
        for b in range(tops):
            bit = LANES.bit_length() - 1 + b - low_bits
            bit = bit if bit < na_bits else bit - na_bits + ROW_HIGH
            flip[b, at_t, :] = sign(code >> bit).astype(jnp.bfloat16)
        odd = col & d
        for b in (4, 2, 1):
            odd = odd ^ odd >> b
        lane[at_t, :LANES] = sign(odd).astype(jnp.bfloat16)
        lane[at_t, LANES:] = sign(odd ^ col >> 7).astype(jnp.bfloat16)
        low[at_t, :] = jnp.where((down(order_ref, t) ^ d) & (LANES - 1) == 0, 1.0, 0.0).astype(jnp.bfloat16)
        high[:, at_t] = jnp.where(order_ref[pl.ds(t, 1), :] >> 7 == coarse, 1.0, 0.0).astype(jnp.bfloat16)
        return carry

    lax.fori_loop(0, key_ref.shape[0], tile, 0, unroll=4)


def slot_factors(key, order, base, na, nh):
    k = key.shape[0]
    tops = (na * nh * LOW // LANES).bit_length() - 1
    tiles = 8
    parts = k // TILE // tiles
    some = lambda *shape: jax.ShapeDtypeStruct(shape, jnp.bfloat16)
    rows = lambda width: pl.BlockSpec((k // parts, width), lambda i, *s: (i, 0))
    ids = pl.BlockSpec((tiles, LANES), lambda i, *s: (i, 0))
    return pl.pallas_call(
        functools.partial(factor_body, na, tops),
        out_shape=[some(k, LANES), some(max(tops, 1), k, LANES), some(k, BLK), some(k, LANES), some(k // LANES, k)],
        grid_spec=pltpu.PrefetchScalarGridSpec(
            num_scalar_prefetch=1,
            grid=(parts,),
            in_specs=[ids, ids],
            out_specs=[
                rows(LANES),
                pl.BlockSpec((max(tops, 1), k // parts, LANES), lambda i, *s: (0, i, 0)),
                rows(BLK),
                rows(LANES),
                pl.BlockSpec((k // LANES, k // parts), lambda i, *s: (0, i)),
            ],
        ),
        compiler_params=pltpu.CompilerParams(vmem_limit_bytes=60 << 20),
        cost_estimate=pl.CostEstimate(flops=80 * k * LANES, bytes_accessed=2 * k * LANES * 8, transcendentals=0),
    )(base, key.reshape(k // LANES, LANES), order.reshape(k // LANES, LANES))


def halve(x):
    coarse = x.astype(jnp.bfloat16)
    return coarse, (x - coarse.astype(jnp.float32)).astype(jnp.bfloat16)


def body(parts, na, nc, steps, tops, unroll, ends, place, a_ref, *refs):
    g_refs = refs[:parts]
    words_ref, h_ref, pick_hbm, flip_hbm, lane_hbm, low_hbm, high_ref, out_ref, at, w, pick, flip, lane, low, part, spread, sems = refs[parts:]
    step = pl.program_id(0)
    pairs = ((pick_hbm, pick), (flip_hbm, flip), (lane_hbm, lane), (low_hbm, low))
    copies = [pltpu.make_async_copy(s, d, sems.at[i]) for i, (s, d) in enumerate(pairs)]

    @pl.when(step == 0)
    def _():
        for c in copies:
            c.start()
        blocks, _, _, span = a_ref.shape
        for j in range(blocks):
            tokens = jnp.concatenate([a_ref[j, place[0] ^ s] for s in range(parts)], axis=0)
            at[j * span:(j + 1) * span, :] = tokens.T

    depth = na * LOW
    shift = 31 - lax.broadcasted_iota(jnp.int32, (BLK // 16, 16, BLK), 1)
    for c in range(nc):
        cols = slice(c * BLK, (c + 1) * BLK)
        grads_out = jnp.concatenate([g[:, cols] for g in g_refs], axis=0)
        for a in range(0, na, 2):
            halves = []
            for b in (a, a + 1):
                rows = slice(b * BLK, (b + 1) * BLK)
                grad = jnp.dot(at[rows, :], grads_out, preferred_element_type=jnp.float32)
                words = words_ref[b * BLK // 16:(b + 1) * BLK // 16, cols]
                marks = (jnp.broadcast_to(words[:, None, :], shift.shape) << shift).reshape(BLK, BLK)
                signed = jnp.where(marks < 0, -grad, grad).astype(jnp.bfloat16)
                mixed = jnp.dot(h_ref[...], signed, preferred_element_type=jnp.float32)
                halves.append(mixed.reshape(GROUPS, LOW, BLK))
            both = jnp.concatenate(halves, axis=1).astype(jnp.bfloat16)
            w[:, pl.ds(pl.multiple_of((step * nc + c) * depth + a * LOW, 2 * LOW), 2 * LOW), :] = both

    @pl.when(step == steps - 1)
    def _():
        for c in copies:
            c.wait()
        slot = lax.broadcasted_iota(jnp.int32, (TILE, LANES), 0)

        tiles = pick.shape[0] // TILE

        def item(i, carry):
            t, g, start = carry
            at_t = pl.ds(pl.multiple_of(t * TILE, TILE), TILE)
            signs = [pick[at_t, :]]
            for b in range(tops):
                signs += [s * flip[b, at_t, :] for s in signs]
            mixed = jnp.dot(jnp.concatenate(signs, axis=1), w[g], preferred_element_type=jnp.float32)
            mixed = mixed * lane[at_t, :].astype(jnp.float32)
            part[at_t, :] = jnp.where(slot >= start - t * TILE, mixed[:, :LANES] + mixed[:, LANES:], part[at_t, :])
            stop, last = ends[g], (t + 1) * TILE
            onward = (g < GROUPS - 1) & (stop <= last)
            g = jnp.where(onward, g + 1, g)
            t = jnp.minimum(jnp.where(onward, t, t + 1), tiles - 1)
            return t, g, jnp.where(onward, stop, last)

        zero = jnp.int32(0)
        lax.fori_loop(0, tiles + GROUPS - 1, item, (zero, zero, zero), unroll=unroll)
        ones = jnp.ones((LANES, LANES), jnp.bfloat16)

        def back(t, carry):
            at_t = pl.ds(pl.multiple_of(t * TILE, TILE), TILE)
            value = sum(jnp.dot(x, ones, preferred_element_type=jnp.float32) for x in halve(part[at_t, :]))
            for i, x in enumerate(halve(value)):
                spread[i, at_t, :] = x * low[at_t, :]
            return carry

        lax.fori_loop(0, high_ref.shape[1] // TILE, back, 0, unroll=32)
        out_ref[...] = sum(jnp.dot(high_ref[...], spread[i], preferred_element_type=jnp.float32) for i in (0, 1))


def sketch_terms(ends, place, panel, example, g_parts, words, h, pick, flip, lane, low_hot, high_hot):
    blocks, parts, few, span = panel.shape
    rows, cols = 16 * words.shape[0], words.shape[1]
    wide = min(cols, WIDE)
    steps = cols // wide
    na, nc = rows // BLK, wide // BLK
    k = pick.shape[0]
    depth = na * nc * steps * LOW
    tops = (depth // LANES).bit_length() - 1
    whole = lambda *shape: pl.BlockSpec(shape, lambda j, *s: (0,) * len(shape))
    hbm = pl.BlockSpec(memory_space=pltpu.HBM)
    return pl.pallas_call(
        functools.partial(body, parts, na, nc, steps, tops, 21),
        out_shape=jax.ShapeDtypeStruct((k // LANES, LANES), jnp.float32),
        grid_spec=pltpu.PrefetchScalarGridSpec(
            num_scalar_prefetch=2,
            grid=(steps,),
            in_specs=[whole(blocks, parts, few, span)]
            + [pl.BlockSpec((None, few, wide), lambda j, *s: (example, 0, j))] * parts
            + [pl.BlockSpec((rows // 16, wide), lambda j, *s: (0, j)), whole(BLK, BLK)]
            + [hbm] * 4
            + [whole(*high_hot.shape)],
            out_specs=whole(k // LANES, LANES),
            scratch_shapes=[
                pltpu.VMEM((rows, parts * few), jnp.bfloat16),
                pltpu.VMEM((GROUPS, depth, BLK), jnp.bfloat16),
                pltpu.VMEM(pick.shape, jnp.bfloat16),
                pltpu.VMEM(flip.shape, jnp.bfloat16),
                pltpu.VMEM(lane.shape, jnp.bfloat16),
                pltpu.VMEM(low_hot.shape, jnp.bfloat16),
                pltpu.VMEM((k, LANES), jnp.float32),
                pltpu.VMEM((2, k, LANES), jnp.bfloat16),
                pltpu.SemaphoreType.DMA((4,)),
            ],
        ),
        compiler_params=pltpu.CompilerParams(vmem_limit_bytes=52 << 20),
        cost_estimate=pl.CostEstimate(
            flops=2 * rows * wide * steps * 3 * BLK, bytes_accessed=2 * rows * wide * steps, transcendentals=0
        ),
    )(ends, place, panel, *g_parts, words, h, pick, flip, lane, low_hot, high_hot)


def local(sizes, share, activations, out_grads, sign_bits, kept_row, kept_col):
    wide_size, narrow_size = sizes["wide"], sizes["narrow"]
    n = lax.axis_index("narrow")
    wide_idx = lax.axis_index("wide")
    count = activations.shape[0]
    row_len = activations.shape[2]
    col_len = out_grads.shape[2] // share
    few = out_grads.shape[1]
    k = kept_row.shape[0]
    na = share * row_len // BLK
    nh = col_len // BLK

    def swap(x, s):
        return lax.ppermute(x, "narrow", [(j, j ^ s) for j in range(narrow_size)])

    def columns(x, s):
        return lax.dynamic_slice_in_dim(x, ((n ^ s) % share) * col_len, col_len, x.ndim - 1)

    def spread(x):
        return [x] + [swap(x, s) for s in range(1, share)]

    def panel(rows):
        return lax.all_gather(jnp.stack(rows), "wide", axis=1, tiled=True).reshape(share, narrow_size, few, row_len)

    near = spread(activations[:2])
    words = [columns(sign_bits, 0)] + [swap(columns(sign_bits, s).astype(jnp.uint16), s) for s in range(1, share)]
    outs = out_grads[:2]
    outs = [columns(outs, 0)] + [swap(columns(outs, s), s) for s in range(1, narrow_size)]
    grads = [(e, outs) for e in range(2)]
    key, order = in_groups(kept_row, kept_col)
    key, order, near = lax.optimization_barrier((key, order, near))
    first = near[-1]
    outs, acts, *_ = lax.optimization_barrier((out_grads[2:], activations[2:], words[-1], first))
    words = jnp.concatenate([x.astype(jnp.int32) for x in words])
    rest = [columns(outs, 0)] + [swap(columns(outs, s), s) for s in range(1, narrow_size)]
    grads += [(e, rest) for e in range(count - 2)]
    panels = [panel([x[e] for x in near]) for e in range(2)]
    far = spread(acts)
    base = n * (row_len // BLK) | ((wide_idx * share + n % share) * nh) << ROW_HIGH
    factors = slot_factors(key, order, jnp.full((1,), base, jnp.int32), na, nh)
    groups = jnp.arange(GROUPS, dtype=jnp.int32)
    ends = jnp.sum(((kept_row & (BLK - 1)) // LOW <= groups[:, None]).astype(jnp.int32), axis=1)
    index = jnp.arange(BLK, dtype=jnp.int32)
    h = parity_sign(index[:, None], index[None, :])
    place = jnp.full((1,), n, jnp.int32)
    terms = []
    for e in range(count):
        if e == 1:
            far, _ = lax.optimization_barrier((far, terms[0]))
            panels += [panel([x[i] for x in far]) for i in range(count - 2)]
        if e:
            ends, _ = lax.optimization_barrier((ends, terms[-1]))
        terms.append(sketch_terms(ends, place, panels[e], *grads[e], words, h, *factors))
    owners = wide_size * narrow_size
    send = jnp.stack(terms).reshape(count, owners, k // owners).transpose(1, 0, 2)
    got = lax.all_to_all(send, ("wide", "narrow"), 0, 0, tiled=True)
    return jnp.sum(got, axis=0) * (1.0 / math.sqrt(D * FF * SEQ))


def solution(mesh):
    return jax.shard_map(
        functools.partial(local, dict(mesh.shape), 2),
        mesh=mesh,
        in_specs=(
            P("groups", "wide", "narrow"),
            P("groups", "narrow", "wide"),
            P("narrow", "wide"),
            P(),
            P(),
        ),
        out_specs=P("groups", ("wide", "narrow")),
        check_vma=False,
    )
```

```python
import functools
import math

import jax
import jax.numpy as jnp
from jax import lax
from jax.experimental import pallas as pl
from jax.experimental.pallas import tpu as pltpu
from jax.sharding import PartitionSpec as P

D = 8192
FF = 16384
SEQ = 128
BLK = 256
LOW = 8
GROUPS = BLK // LOW
LANES = 128
TILE = 128
WIDE = 1024
ROW_HIGH = (D // BLK).bit_length() - 1
COL_BITS = FF.bit_length() - 1


def parity_sign(first, second):
    folded = first & second
    folded = folded ^ folded >> 8
    folded = folded ^ folded >> 4
    folded = folded ^ folded >> 2
    folded = folded ^ folded >> 1
    return (1 - 2 * (folded & 1)).astype(jnp.bfloat16)


def in_groups(kept_row, kept_col):
    key = ((kept_row & (BLK - 1)) << ROW_HIGH | kept_row // BLK) << COL_BITS | kept_col
    return lax.sort((key, lax.iota(jnp.int32, key.shape[0])), num_keys=1)


def factor_body(na, tops, base, key_ref, order_ref, pick, flip, lane, low, high):
    d = lax.broadcasted_iota(jnp.int32, (TILE, LANES), 1)
    low_bits = LOW.bit_length() - 1
    na_bits = na.bit_length() - 1
    place = base[0] ^ ((d >> low_bits) & (na - 1) | d >> (low_bits + na_bits) << ROW_HIGH)
    coarse = lax.broadcasted_iota(jnp.int32, (high.shape[0], LANES), 0)

    def down(ref, t):
        return jnp.broadcast_to(ref[pl.ds(t, 1), :], (TILE, LANES)).T

    def sign(odd):
        return (1 - 2 * (odd & 1)).astype(jnp.float32)

    def tile(t, carry):
        at_t = pl.ds(pl.multiple_of(t * TILE, TILE), TILE)
        key = down(key_ref, t)
        col = key & (FF - 1)
        row_low = key >> (COL_BITS + ROW_HIGH)
        code = (key >> COL_BITS) & (D // BLK - 1) | col // BLK << ROW_HIGH
        odd = code & place
        for b in (8, 4, 2, 1):
            odd = odd ^ odd >> b
        pick[at_t, :] = jnp.where((row_low ^ d) & (LOW - 1) == 0, sign(odd), 0.0).astype(jnp.bfloat16)
        for b in range(tops):
            bit = LANES.bit_length() - 1 + b - low_bits
            bit = bit if bit < na_bits else bit - na_bits + ROW_HIGH
            flip[b, at_t, :] = sign(code >> bit).astype(jnp.bfloat16)
        odd = col & d
        for b in (4, 2, 1):
            odd = odd ^ odd >> b
        lane[at_t, :LANES] = sign(odd).astype(jnp.bfloat16)
        lane[at_t, LANES:] = sign(odd ^ col >> 7).astype(jnp.bfloat16)
        low[at_t, :] = jnp.where((down(order_ref, t) ^ d) & (LANES - 1) == 0, 1.0, 0.0).astype(jnp.bfloat16)
        high[:, at_t] = jnp.where(order_ref[pl.ds(t, 1), :] >> 7 == coarse, 1.0, 0.0).astype(jnp.bfloat16)
        return carry

    lax.fori_loop(0, key_ref.shape[0], tile, 0, unroll=4)


def slot_factors(key, order, base, na, nh):
    k = key.shape[0]
    tops = (na * nh * LOW // LANES).bit_length() - 1
    tiles = 8
    parts = k // TILE // tiles
    some = lambda *shape: jax.ShapeDtypeStruct(shape, jnp.bfloat16)
    rows = lambda width: pl.BlockSpec((k // parts, width), lambda i, *s: (i, 0))
    ids = pl.BlockSpec((tiles, LANES), lambda i, *s: (i, 0))
    return pl.pallas_call(
        functools.partial(factor_body, na, tops),
        out_shape=[some(k, LANES), some(max(tops, 1), k, LANES), some(k, BLK), some(k, LANES), some(k // LANES, k)],
        grid_spec=pltpu.PrefetchScalarGridSpec(
            num_scalar_prefetch=1,
            grid=(parts,),
            in_specs=[ids, ids],
            out_specs=[
                rows(LANES),
                pl.BlockSpec((max(tops, 1), k // parts, LANES), lambda i, *s: (0, i, 0)),
                rows(BLK),
                rows(LANES),
                pl.BlockSpec((k // LANES, k // parts), lambda i, *s: (0, i)),
            ],
        ),
        compiler_params=pltpu.CompilerParams(vmem_limit_bytes=60 << 20),
        cost_estimate=pl.CostEstimate(flops=80 * k * LANES, bytes_accessed=2 * k * LANES * 8, transcendentals=0),
    )(base, key.reshape(k // LANES, LANES), order.reshape(k // LANES, LANES))


def halve(x):
    coarse = x.astype(jnp.bfloat16)
    return coarse, (x - coarse.astype(jnp.float32)).astype(jnp.bfloat16)


def body(parts, na, nc, steps, tops, unroll, ends, place, a_ref, *refs):
    g_refs = refs[:parts]
    words_ref, h_ref, pick_hbm, flip_hbm, lane_hbm, low_hbm, high_ref, out_ref, at, w, pick, flip, lane, low, part, spread, sems = refs[parts:]
    step = pl.program_id(0)
    pairs = ((pick_hbm, pick), (flip_hbm, flip), (lane_hbm, lane), (low_hbm, low))
    copies = [pltpu.make_async_copy(s, d, sems.at[i]) for i, (s, d) in enumerate(pairs)]

    @pl.when(step == 0)
    def _():
        for c in copies:
            c.start()
        blocks, _, _, span = a_ref.shape
        for j in range(blocks):
            tokens = jnp.concatenate([a_ref[j, place[0] ^ s] for s in range(parts)], axis=0)
            at[j * span:(j + 1) * span, :] = tokens.T

    depth = na * LOW
    shift = 31 - lax.broadcasted_iota(jnp.int32, (BLK // 16, 16, BLK), 1)
    for c in range(nc):
        cols = slice(c * BLK, (c + 1) * BLK)
        grads_out = jnp.concatenate([g[:, cols] for g in g_refs], axis=0)
        for a in range(0, na, 2):
            halves = []
            for b in (a, a + 1):
                rows = slice(b * BLK, (b + 1) * BLK)
                grad = jnp.dot(at[rows, :], grads_out, preferred_element_type=jnp.float32)
                words = words_ref[b * BLK // 16:(b + 1) * BLK // 16, cols]
                marks = (jnp.broadcast_to(words[:, None, :], shift.shape) << shift).reshape(BLK, BLK)
                signed = jnp.where(marks < 0, -grad, grad).astype(jnp.bfloat16)
                mixed = jnp.dot(h_ref[...], signed, preferred_element_type=jnp.float32)
                halves.append(mixed.reshape(GROUPS, LOW, BLK))
            both = jnp.concatenate(halves, axis=1).astype(jnp.bfloat16)
            w[:, pl.ds(pl.multiple_of((step * nc + c) * depth + a * LOW, 2 * LOW), 2 * LOW), :] = both

    @pl.when(step == steps - 1)
    def _():
        for c in copies:
            c.wait()
        slot = lax.broadcasted_iota(jnp.int32, (TILE, LANES), 0)

        tiles = pick.shape[0] // TILE

        def item(i, carry):
            t, g, start = carry
            at_t = pl.ds(pl.multiple_of(t * TILE, TILE), TILE)
            signs = [pick[at_t, :]]
            for b in range(tops):
                signs += [s * flip[b, at_t, :] for s in signs]
            mixed = jnp.dot(jnp.concatenate(signs, axis=1), w[g], preferred_element_type=jnp.float32)
            mixed = mixed * lane[at_t, :].astype(jnp.float32)
            part[at_t, :] = jnp.where(slot >= start - t * TILE, mixed[:, :LANES] + mixed[:, LANES:], part[at_t, :])
            stop, last = ends[g], (t + 1) * TILE
            onward = (g < GROUPS - 1) & (stop <= last)
            g = jnp.where(onward, g + 1, g)
            t = jnp.minimum(jnp.where(onward, t, t + 1), tiles - 1)
            return t, g, jnp.where(onward, stop, last)

        zero = jnp.int32(0)
        lax.fori_loop(0, tiles + GROUPS - 1, item, (zero, zero, zero), unroll=unroll)
        ones = jnp.ones((LANES, LANES), jnp.bfloat16)

        def back(t, carry):
            at_t = pl.ds(pl.multiple_of(t * TILE, TILE), TILE)
            value = sum(jnp.dot(x, ones, preferred_element_type=jnp.float32) for x in halve(part[at_t, :]))
            for i, x in enumerate(halve(value)):
                spread[i, at_t, :] = x * low[at_t, :]
            return carry

        lax.fori_loop(0, high_ref.shape[1] // TILE, back, 0, unroll=32)
        out_ref[...] = sum(jnp.dot(high_ref[...], spread[i], preferred_element_type=jnp.float32) for i in (0, 1))


def sketch_terms(ends, place, panel, example, g_parts, words, h, pick, flip, lane, low_hot, high_hot):
    blocks, parts, few, span = panel.shape
    rows, cols = 16 * words.shape[0], words.shape[1]
    wide = min(cols, WIDE)
    steps = cols // wide
    na, nc = rows // BLK, wide // BLK
    k = pick.shape[0]
    depth = na * nc * steps * LOW
    tops = (depth // LANES).bit_length() - 1
    whole = lambda *shape: pl.BlockSpec(shape, lambda j, *s: (0,) * len(shape))
    hbm = pl.BlockSpec(memory_space=pltpu.HBM)
    return pl.pallas_call(
        functools.partial(body, parts, na, nc, steps, tops, 21),
        out_shape=jax.ShapeDtypeStruct((k // LANES, LANES), jnp.float32),
        grid_spec=pltpu.PrefetchScalarGridSpec(
            num_scalar_prefetch=2,
            grid=(steps,),
            in_specs=[whole(blocks, parts, few, span)]
            + [pl.BlockSpec((None, few, wide), lambda j, *s: (example, 0, j))] * parts
            + [pl.BlockSpec((rows // 16, wide), lambda j, *s: (0, j)), whole(BLK, BLK)]
            + [hbm] * 4
            + [whole(*high_hot.shape)],
            out_specs=whole(k // LANES, LANES),
            scratch_shapes=[
                pltpu.VMEM((rows, parts * few), jnp.bfloat16),
                pltpu.VMEM((GROUPS, depth, BLK), jnp.bfloat16),
                pltpu.VMEM(pick.shape, jnp.bfloat16),
                pltpu.VMEM(flip.shape, jnp.bfloat16),
                pltpu.VMEM(lane.shape, jnp.bfloat16),
                pltpu.VMEM(low_hot.shape, jnp.bfloat16),
                pltpu.VMEM((k, LANES), jnp.float32),
                pltpu.VMEM((2, k, LANES), jnp.bfloat16),
                pltpu.SemaphoreType.DMA((4,)),
            ],
        ),
        compiler_params=pltpu.CompilerParams(vmem_limit_bytes=52 << 20),
        cost_estimate=pl.CostEstimate(
            flops=2 * rows * wide * steps * 3 * BLK, bytes_accessed=2 * rows * wide * steps, transcendentals=0
        ),
    )(ends, place, panel, *g_parts, words, h, pick, flip, lane, low_hot, high_hot)


def local(sizes, share, activations, out_grads, sign_bits, kept_row, kept_col):
    wide_size, narrow_size = sizes["wide"], sizes["narrow"]
    n = lax.axis_index("narrow")
    wide_idx = lax.axis_index("wide")
    count = activations.shape[0]
    row_len = activations.shape[2]
    col_len = out_grads.shape[2] // share
    few = out_grads.shape[1]
    k = kept_row.shape[0]
    na = share * row_len // BLK
    nh = col_len // BLK

    def swap(x, s):
        return lax.ppermute(x, "narrow", [(j, j ^ s) for j in range(narrow_size)])

    def columns(x, s):
        return lax.dynamic_slice_in_dim(x, ((n ^ s) % share) * col_len, col_len, x.ndim - 1)

    def spread(x):
        return [x] + [swap(x, s) for s in range(1, share)]

    def panel(rows):
        return lax.all_gather(jnp.stack(rows), "wide", axis=1, tiled=True).reshape(share, narrow_size, few, row_len)

    near = spread(activations[:2])
    words = [columns(sign_bits, 0)] + [swap(columns(sign_bits, s).astype(jnp.uint16), s) for s in range(1, share)]
    outs = out_grads[:2]
    outs = [columns(outs, 0)] + [swap(columns(outs, s), s) for s in range(1, narrow_size)]
    grads = [(e, outs) for e in range(2)]
    key, order = in_groups(kept_row, kept_col)
    key, order, near = lax.optimization_barrier((key, order, near))
    first = near[-1]
    outs, acts, *_ = lax.optimization_barrier((out_grads[2:], activations[2:], words[-1], first))
    words = jnp.concatenate([x.astype(jnp.int32) for x in words])
    rest = [columns(outs, 0)] + [swap(columns(outs, s), s) for s in range(1, narrow_size)]
    grads += [(e, rest) for e in range(count - 2)]
    panels = [panel([x[e] for x in near]) for e in range(2)]
    far = spread(acts)
    base = n * (row_len // BLK) | ((wide_idx * share + n % share) * nh) << ROW_HIGH
    factors = slot_factors(key, order, jnp.full((1,), base, jnp.int32), na, nh)
    groups = jnp.arange(GROUPS, dtype=jnp.int32)
    ends = jnp.sum(((kept_row & (BLK - 1)) // LOW <= groups[:, None]).astype(jnp.int32), axis=1)
    index = jnp.arange(BLK, dtype=jnp.int32)
    h = parity_sign(index[:, None], index[None, :])
    place = jnp.full((1,), n, jnp.int32)
    terms = []
    for e in range(count):
        if e == 1:
            far, _ = lax.optimization_barrier((far, terms[0]))
            panels += [panel([x[i] for x in far]) for i in range(count - 2)]
        if e:
            ends, _ = lax.optimization_barrier((ends, terms[-1]))
        terms.append(sketch_terms(ends, place, panels[e], *grads[e], words, h, *factors))
    owners = wide_size * narrow_size
    send = jnp.stack(terms).reshape(count, owners, k // owners).transpose(1, 0, 2)
    got = lax.all_to_all(send, ("wide", "narrow"), 0, 0, tiled=True)
    return jnp.sum(got, axis=0) * (1.0 / math.sqrt(D * FF * SEQ))


def solution(mesh):
    return jax.shard_map(
        functools.partial(local, dict(mesh.shape), 2),
        mesh=mesh,
        in_specs=(
            P("groups", "wide", "narrow"),
            P("groups", "narrow", "wide"),
            P("narrow", "wide"),
            P(),
            P(),
        ),
        out_specs=P("groups", ("wide", "narrow")),
        check_vma=False,
    )
```
